256 devices in a mesh: rows: 32 (over z, y), rhs: 8 (over x, core).
Axes of the slice: x: 4, y: 4, z: 8, core: 2. Of those that a mesh axis runs over, the one named last changes fastest.
Arguments:
- x_t: bfloat16 [64, 131072], P('rhs', 'rows'), may hold values from -6 to 6
- far_v: bfloat16 [32, 64, 64, 512], P('rows', 'rhs'), may hold values from -0.25 to 0.25
- far_u: bfloat16 [32, 64, 64, 4096], P('rows', 'rhs'), may hold values from -0.125 to 0.125
- far_cols: int32 [32, 64], P('rows', 'rhs'), may hold values from 0 to 255, as said below
- rank_class: int32 [32, 64], P('rows', 'rhs'), may hold values from 0 to 2
- near_block: bfloat16 [131072, 4096], P('rows', 'rhs'), may hold values from -0.09375 to 0.09375
Outputs:
- y_t: bfloat16 [64, 131072], P('rhs', 'rows')
The draws below stay inside these ranges and needn't reach their ends.
Inputs may be any that keep to these rules, and one draw needn't show every extreme that they name: For k * 8 <= b < (k + 1) * 8, far_cols[i, b] * 512 lies in [k * 16384, (k + 1) * 16384) and outside [i * 4096, (i + 1) * 4096); no value repeats within a row cluster.
All inputs are finite; a program needn't handle non-finite values.
Results may differ from the reference program's by a relative error of at most 0.0043.
Values may be sent and summed in bfloat16 or wider, within the bound.
No kernel may reach another device: no remote copies, remote signals or barrier semaphores. Data moves between devices by JAX's collectives and lax.ppermute only.
A program may use at most 128 MiB of HBM per device.

```python
import jax
import jax.numpy as jnp
from jax import lax

S = 4096
NRHS = 64
RMAX = 64
PIECES = 8
BLK = 8
CLUSTERS = 32
FAR = 64
W = 512
N = 131072


def draw_far_cols(key, part):
    key = jax.random.fold_in(key, 7)
    devices_rhs = FAR // BLK
    group_size = CLUSTERS // devices_rhs
    candidates = group_size * PIECES
    positions = jnp.arange(candidates, dtype=jnp.int32)

    def one_device(cluster_id, column_group):
        sub_key = jax.random.fold_in(jax.random.fold_in(key, cluster_id), column_group)
        scores = jax.random.permutation(sub_key, candidates).astype(jnp.int32)
        owner_ids = positions // PIECES + column_group * group_size
        scores = jnp.where(owner_ids == cluster_id, scores + candidates, scores)
        first_hit = (cluster_id == CLUSTERS - 1) & (column_group == 0) & (positions == 0)
        last_hit = (cluster_id == 0) & (column_group == devices_rhs - 1) & (positions == candidates - 1)
        scores = jnp.where(first_hit | last_hit, -1, scores)
        chosen = jnp.argsort(scores, stable=True)[:BLK]
        return (chosen + column_group * candidates).astype(jnp.int32)
    cluster_ids = jnp.arange(CLUSTERS, dtype=jnp.int32)
    group_ids = jnp.arange(devices_rhs, dtype=jnp.int32)
    block_table = jax.vmap(lambda cluster_id: jax.vmap(lambda group_id: one_device(cluster_id, group_id))(group_ids))(cluster_ids)
    return block_table.reshape(CLUSTERS, FAR).astype(jnp.int32)


def draw_rank_class(key, part):
    key = jax.random.fold_in(key, 11)
    level_key, block_key = jax.random.split(key)
    devices_rhs = FAR // BLK
    device_level = jax.random.randint(level_key, (CLUSTERS, devices_rhs, 1), 0, 3)
    block_extra = jax.random.randint(block_key, (CLUSTERS, devices_rhs, BLK), 0, 2)
    return jnp.minimum(device_level + block_extra, 2).reshape(CLUSTERS, FAR).astype(jnp.int32)


def levels(own_key, shape, pieces, smallest, top_value):
    loudness = 1.0
    for dim, blocks in pieces:
        heights = jax.random.uniform(jax.random.fold_in(jax.random.fold_in(own_key, 6), dim), (blocks,), jnp.float32, smallest / len(pieces), top_value / len(pieces))
        loudness = loudness * jnp.repeat(jnp.exp(heights), shape[dim] // blocks).reshape((-1,) + (1,) * (len(shape) - 1 - dim))
    return loudness


def centred(key, extent, scale, limit, cuts=(), kind=jnp.bfloat16):
    array = jax.random.normal(key, extent, jnp.float32) * scale
    if len(cuts) > 0:
        array = levels(key, extent, cuts, -0.22, 0.18) * array
    return jnp.clip(array, min=-limit, max=limit).astype(kind)


def setup_inputs(seed: int = 0) -> dict:
    key_of = jax.random.split(jax.random.key(seed), 7)
    return {
        "x_t": centred(key_of[0], (NRHS, N), 1.0, 6.0, ((0, 8), (1, 32))),
        "far_v": centred(key_of[1], (CLUSTERS, FAR, RMAX, W), W ** -0.5, 0.25, ((0, 32), (1, 8))),
        "far_u": centred(key_of[2], (CLUSTERS, FAR, RMAX, S), (RMAX * FAR // 2) ** -0.5, 0.125, ((0, 32), (1, 8))),
        "far_cols": draw_far_cols(jax.random.fold_in(key_of[6], 71), 0),
        "rank_class": draw_rank_class(jax.random.fold_in(key_of[6], 71), 0),
        "near_block": centred(key_of[5], (N, S), S ** -0.5, 0.09375, ((0, 32), (1, 8))),
    }


def reference(x_t, far_v, far_u, far_cols, rank_class, near_block):
    def one_cluster(cluster_id):
        column_ids = far_cols[cluster_id]
        classes = rank_class[cluster_id]
        blocks = jax.vmap(lambda column_id: lax.dynamic_slice_in_dim(x_t, (column_id * W).astype(jnp.int32), W, 1))(column_ids)
        coeffs = jnp.einsum('brt,bct->brc', far_v[cluster_id].astype(jnp.float32), blocks.astype(jnp.float32))
        rank_cut = jnp.where(classes == 0, RMAX // 4, jnp.where(classes == 1, RMAX // 2, RMAX))
        keep_mask = jnp.arange(RMAX, dtype=jnp.int32)[None, :, None] < rank_cut[:, None, None]
        coeffs = jnp.where(keep_mask, coeffs, jnp.float32(0.0)).astype(jnp.bfloat16)
        far_part = jnp.einsum('brs,brc->cs', far_u[cluster_id].astype(jnp.float32), coeffs.astype(jnp.float32))
        first_row = (cluster_id * S).astype(jnp.int32)
        own_cols = lax.dynamic_slice_in_dim(x_t, first_row, S, 1)
        dense_rows = lax.dynamic_slice_in_dim(near_block, first_row, S, 0)
        near_part = jnp.einsum('ct,st->cs', own_cols.astype(jnp.float32), dense_rows.astype(jnp.float32))
        return (far_part + near_part).astype(jnp.bfloat16)

    results = lax.map(one_cluster, jnp.arange(CLUSTERS, dtype=jnp.int32))
    return jnp.transpose(results, (1, 0, 2)).reshape(NRHS, N)
```

```python
import jax
import jax.numpy as jnp
from jax import lax
from jax.experimental import pallas as pl
from jax.experimental.pallas import tpu as pltpu
from jax.sharding import PartitionSpec as P

Z, Y, X, C = 8, 4, 4, 2
PIECES, BLK, RANK, W, S = 8, 8, 64, 512, 4096
AXES = ("rows", "rhs")
NT = (((1,), (1,)), ((), ()))
NN = (((1,), (0,)), ((), ()))
TILE = 512
VMEM, SMEM = pl.BlockSpec(memory_space=pltpu.VMEM), pl.BlockSpec(memory_space=pltpu.SMEM)
ORDER = (5, 3, 4, 6, 2, 7, 1, 0)
LONG = pl.CostEstimate(flops=20 << 30, bytes_accessed=1 << 20, transcendentals=0)
LIMIT = pltpu.CompilerParams(vmem_limit_bytes=8 << 20)


def bf16(*shape):
    return jax.ShapeDtypeStruct(shape, jnp.bfloat16)


def f32(*shape):
    return jax.ShapeDtypeStruct(shape, jnp.float32)


def pairs(target):
    place = lambda z, y, x, c: ((z * Y + y) * X + x) * C + c
    return [
        (place(z, y, x, c), place(*target(z, y, x, c)))
        for z in range(Z) for y in range(Y) for x in range(X) for c in range(C)
    ]


def move(part, target):
    return lax.ppermute(part, AXES, pairs(target))


def along_x(part, m):
    return part if m == 0 else move(part, lambda z, y, x, c: (z, y, (x + m) % X, c))


def along_y(part, m):
    return part if m == 0 else move(part, lambda z, y, x, c: (z, (y + m) % Y, x, c))


def along_z(part, m):
    return part if m == 0 else move(part, lambda z, y, x, c: ((z + m) % Z, y, x, c))


def other_core(part):
    return move(part, lambda z, y, x, c: (z, y, x, 1 - c))


def pick_kernel(*refs):
    held_refs, table_ref, out_refs, held_ref = refs[:Y], refs[Y], refs[Y + 1:-1], refs[-1]
    y, z = lax.axis_index("rows") & 3, lax.axis_index("rows") >> 2
    for m in range(Y):
        held_ref[m] = held_refs[m][...]
    for m in range(Z):
        for b in range(BLK):
            piece = table_ref[(z + m) & 7, 0, b]
            source = (y - (piece >> 3)) & 3
            out_refs[m][b] = held_ref[source, :, pl.ds(pl.multiple_of((piece & 7) * W, W), W)]


def pick(table, held):
    return pl.pallas_call(
        pick_kernel,
        out_shape=[bf16(BLK, 8, W)] * Z,
        in_specs=[VMEM] * Y + [SMEM],
        out_specs=[VMEM] * Z,
        scratch_shapes=[pltpu.VMEM((Y, 8, PIECES * W), jnp.bfloat16)],
        compiler_params=LIMIT,
        cost_estimate=LONG,
        name="pick",
    )(*held, table)


def halves_kernel(cols_ref, x_ref, table_ref, mine_ref, yours_ref):
    table_ref[...] = jnp.zeros_like(table_ref)
    table_ref[:, :, :BLK] = jnp.broadcast_to(cols_ref[...], (Z, 1, BLK))
    k = lax.axis_index("rhs")
    x, core = k >> 1, k & 1
    for m in range(X):
        for c, ref in ((core, mine_ref), (1 - core, yours_ref)):
            start = pl.multiple_of((((x + m) & 3) * 2 + c) * W, W)
            ref[m] = x_ref[:, pl.ds(start, W)]


def halves(far_cols, x_t):
    return pl.pallas_call(
        halves_kernel,
        out_shape=[jax.ShapeDtypeStruct((Z, 1, 128), jnp.int32)] + [bf16(X, 8, W)] * 2,
        in_specs=[VMEM] * 2,
        out_specs=[VMEM] * 3,
        compiler_params=LIMIT,
        cost_estimate=LONG,
        name="halves",
    )(far_cols, x_t)


def own_piece(mine, yours):
    theirs = other_core(yours)
    parts = [along_x(jnp.stack([mine[m], theirs[m]]), m) for m in range(X)]
    return [parts[-p % X] for p in range(X)]


def product_kernel(cls_ref, *refs):
    got_refs, own_refs, (v_ref, near_ref, u_ref, keep_ref, send_ref, z_buf) = refs[:Z], refs[Z:Z + X], refs[Z + X:]
    k, depth = lax.axis_index("rhs"), lax.axis_index("rows") >> 2
    x, core = k >> 1, k & 1
    got = [got_refs[ORDER.index(m)] for m in range(Z)]
    ranks = lax.broadcasted_iota(jnp.int32, (64, RANK), 1)
    halves = []
    for b in range(BLK):
        block = jnp.concatenate([r[b].astype(jnp.float32) for r in got], 0).astype(jnp.bfloat16)
        z = lax.dot_general(block, v_ref[b], NT, preferred_element_type=jnp.float32)
        rank = jnp.where(cls_ref[b] == 0, RANK // 4, jnp.where(cls_ref[b] == 1, RANK // 2, RANK))
        halves.append(jnp.where(ranks < rank, z, 0.0))
    for b in range(0, BLK, 2):
        z_buf[b // 2] = jnp.concatenate(halves[b:b + 2], 1).reshape(8, 8, 2 * RANK)
    order = [((x + p) & 3) * 2 + core for p in range(X)] + [((x + p) & 3) * 2 + 1 - core for p in range(X)]
    zmask = jnp.concatenate(
        [jnp.concatenate([z_buf[j, (depth - place) & 7] for place in order], 0) for j in range(BLK // 2)], 1
    ).astype(jnp.bfloat16)
    own = jnp.concatenate([r[c].astype(jnp.float32) for c in range(C) for r in own_refs], 0).astype(jnp.bfloat16)
    for t in range(0, S, TILE):
        cols = slice(t, t + TILE)
        y = lax.dot_general(own, near_ref[cols, :], NT, preferred_element_type=jnp.float32)
        y += lax.dot_general(zmask, u_ref[:, cols], NN, preferred_element_type=jnp.float32)
        keep_ref[:, cols] = y[:32]
        send_ref[:, cols] = y[32:].astype(jnp.bfloat16)


def product(classes, got, own, v, near, u):
    return pl.pallas_call(
        product_kernel,
        out_shape=(f32(32, S), bf16(32, S)),
        in_specs=[SMEM] + [VMEM] * (Z + X + 3),
        out_specs=(VMEM, VMEM),
        scratch_shapes=[pltpu.VMEM((BLK // 2, 8, 8, 2 * RANK), jnp.float32)],
        compiler_params=LIMIT,
        cost_estimate=pl.CostEstimate(flops=4 * 64 * W * S, bytes_accessed=10 << 20, transcendentals=0),
        name="product",
    )(classes, *got, *own, v, near, u)


def on_device(x_t, far_v, far_u, far_cols, rank_class, near_block):
    asked, kept, given = halves(far_cols, x_t)
    mine = move(x_t, lambda z, y, x, c: (2 * x + c, y, z // 2, z % 2))
    lines = [[z * Y + y for z in range(Z)] for y in range(Y)]
    table = lax.all_to_all(asked, "rows", 0, 0, axis_index_groups=lines, tiled=True)
    mine, table = lax.optimization_barrier((mine, table))
    sent = pick(table, [along_y(mine, m) for m in range(Y)])
    own = own_piece(kept, given)
    got = [along_z(sent[m], m) for m in ORDER]
    keep, send = product(
        rank_class.reshape(BLK), got, own, far_v.reshape(BLK, RANK, W), near_block, far_u.reshape(BLK * RANK, S)
    )
    both = keep + other_core(send).astype(jnp.float32)
    parts = [along_x(both[8 * m:8 * m + 8].astype(jnp.bfloat16), m) for m in (2, 1, 3)]
    total = both[:8]
    for part in parts:
        total = total + part.astype(jnp.float32)
    return total.astype(jnp.bfloat16)


def solution(mesh):
    in_specs = (
        P("rhs", "rows"),
        P("rows", "rhs", None, None),
        P("rows", "rhs", None, None),
        P("rows", "rhs"),
        P("rows", "rhs"),
        P("rows", "rhs"),
    )
    return jax.shard_map(on_device, mesh=mesh, in_specs=in_specs, out_specs=P("rhs", "rows"), check_vma=False)
```

```python
import jax
import jax.numpy as jnp
from jax import lax
from jax.experimental import pallas as pl
from jax.experimental.pallas import tpu as pltpu
from jax.sharding import PartitionSpec as P

Z, Y, X, C = 8, 4, 4, 2
PIECES, BLK, RANK, W, S = 8, 8, 64, 512, 4096
AXES = ("rows", "rhs")
NT = (((1,), (1,)), ((), ()))
NN = (((1,), (0,)), ((), ()))
TILE = 512
VMEM, SMEM = pl.BlockSpec(memory_space=pltpu.VMEM), pl.BlockSpec(memory_space=pltpu.SMEM)
TURNS = (0, 4)
SENDS = ((0, (0, 1)), (1, (0, 1)), (-1, (0, 1)), (2, (0,)), (-2, (0,)))
TABLE = 16
LONG = pl.CostEstimate(flops=20 << 30, bytes_accessed=1 << 20, transcendentals=0)
LIMIT = pltpu.CompilerParams(vmem_limit_bytes=8 << 20)


def bf16(*shape):
    return jax.ShapeDtypeStruct(shape, jnp.bfloat16)


def f32(*shape):
    return jax.ShapeDtypeStruct(shape, jnp.float32)


def pairs(target):
    place = lambda z, y, x, c: ((z * Y + y) * X + x) * C + c
    return [
        (place(z, y, x, c), place(*target(z, y, x, c)))
        for z in range(Z) for y in range(Y) for x in range(X) for c in range(C)
    ]


def move(part, target):
    return lax.ppermute(part, AXES, pairs(target))


def across_x(part, j):
    return move(part, lambda z, y, x, c: (z, y, x ^ j, c))


def along_y(part, m):
    return part if m == 0 else move(part, lambda z, y, x, c: (z, (y + m) % Y, x, c))


def along_z(part, m):
    return part if m == 0 else move(part, lambda z, y, x, c: ((z + m) % Z, y, x, c))


def other_core(part):
    return move(part, lambda z, y, x, c: (z, y, x, 1 - c))


def pick_kernel(*refs):
    held_refs, asked_ref, out_refs = refs[:Y], refs[Y], refs[Y + 1:-3]
    held_ref, table_ref, sem = refs[-3:]
    copy = pltpu.make_async_copy(asked_ref.at[:, 0], table_ref, sem)
    copy.start()
    row = lax.axis_index("rows")
    y, z = row & 3, row >> 2
    for m in range(Y):
        held_ref[m] = held_refs[m][...]
    copy.wait()
    for (way, parts), out_ref in zip(SENDS, out_refs):
        for b in range(BLK):
            piece = table_ref[(z + way) & 7, b]
            source = (y - (piece >> 3)) & 3
            cols = pl.ds(pl.multiple_of((piece & 7) * W, W), W)
            for n, part in enumerate(parts):
                out_ref[n, b] = held_ref[source, part, :, cols]


def pick(held, asked):
    return pl.pallas_call(
        pick_kernel,
        out_shape=[bf16(len(parts), BLK, 8, W) for _, parts in SENDS],
        in_specs=[VMEM] * Y + [pl.BlockSpec(memory_space=pl.ANY)],
        out_specs=[VMEM] * len(SENDS),
        scratch_shapes=[
            pltpu.VMEM((Y, len(TURNS), 8, PIECES * W), jnp.bfloat16),
            pltpu.SMEM((Z, 128), jnp.int32),
            pltpu.SemaphoreType.DMA,
        ],
        compiler_params=LIMIT,
        cost_estimate=LONG,
        name="pick",
    )(*held, asked)


def halves_kernel(cols_ref, x_ref, table_ref, mine_ref, yours_ref):
    table_ref[...] = jnp.zeros_like(table_ref)
    table_ref[:, :1, :BLK] = jnp.broadcast_to(cols_ref[...], (Z, 1, BLK))
    k = lax.axis_index("rhs")
    x, core = k >> 1, k & 1
    for j in range(X):
        for c, ref in ((core, mine_ref), (1 - core, yours_ref)):
            start = pl.multiple_of(((x ^ j) * 2 + c) * W, W)
            ref[j] = x_ref[:, pl.ds(start, W)]


def halves(far_cols, x_t):
    return pl.pallas_call(
        halves_kernel,
        out_shape=[jax.ShapeDtypeStruct((Z, TABLE, 128), jnp.int32)] + [bf16(X, 8, W)] * 2,
        in_specs=[VMEM] * 2,
        out_specs=[VMEM] * 3,
        compiler_params=LIMIT,
        cost_estimate=LONG,
        name="halves",
    )(far_cols, x_t)


def own_piece(mine, yours):
    parts = jnp.stack([mine, other_core(yours)], 1)
    far = across_x(parts[2:], 2)
    near = across_x(jnp.stack([parts[1], far[1]]), 1)
    return [parts[0], near[0], far[0], near[1]]


def near_kernel(*refs):
    x_refs, (near_ref, out_ref) = refs[:-2], refs[-2:]
    x = jnp.concatenate([r[c].astype(jnp.float32) for c in range(C) for r in x_refs], 0).astype(jnp.bfloat16)
    for t in range(0, S, TILE):
        out_ref[:, t:t + TILE] = lax.dot_general(
            x, near_ref[t:t + TILE, :], NT, preferred_element_type=jnp.float32
        )


def near_product(own, near):
    return pl.pallas_call(
        near_kernel,
        out_shape=f32(64, S),
        in_specs=[VMEM] * (X + 1),
        out_specs=VMEM,
        compiler_params=LIMIT,
        cost_estimate=pl.CostEstimate(flops=2 * 64 * W * S, bytes_accessed=5 << 20, transcendentals=0),
        name="near",
    )(*own, near)


def product_kernel(cls_ref, *refs):
    got_refs, (v_ref, near_ref, u_ref, keep_ref, send_ref, z_buf) = refs[:len(SENDS)], refs[len(SENDS):]
    k, depth = lax.axis_index("rhs"), lax.axis_index("rows") >> 2
    x, core = k >> 1, k & 1
    got = {
        (-way - TURNS[part]) & 7: (ref, n)
        for ref, (way, parts) in zip(got_refs, SENDS) for n, part in enumerate(parts)
    }
    ranks = lax.broadcasted_iota(jnp.int32, (64, RANK), 1)
    halves = []
    for b in range(BLK):
        block = jnp.concatenate([got[d][0][got[d][1], b].astype(jnp.float32) for d in range(Z)], 0).astype(jnp.bfloat16)
        z = lax.dot_general(block, v_ref[b], NT, preferred_element_type=jnp.float32)
        rank = jnp.where(cls_ref[b] == 0, RANK // 4, jnp.where(cls_ref[b] == 1, RANK // 2, RANK))
        halves.append(jnp.where(ranks < rank, z, 0.0))
    for b in range(0, BLK, 2):
        z_buf[b // 2] = jnp.concatenate(halves[b:b + 2], 1).reshape(8, 8, 2 * RANK)
    order = [(x ^ j) * 2 + core for j in range(X)] + [(x ^ j) * 2 + 1 - core for j in range(X)]
    zmask = jnp.concatenate(
        [jnp.concatenate([z_buf[j, (place - depth) & 7] for place in order], 0) for j in range(BLK // 2)], 1
    ).astype(jnp.bfloat16)
    for t in range(0, S, TILE):
        cols = slice(t, t + TILE)
        y = near_ref[:, cols] + lax.dot_general(zmask, u_ref[:, cols], NN, preferred_element_type=jnp.float32)
        keep_ref[:, cols] = y[:32]
        send_ref[:, cols] = y[32:].astype(jnp.bfloat16)


def product(classes, got, v, near, u):
    return pl.pallas_call(
        product_kernel,
        out_shape=(f32(32, S), bf16(32, S)),
        in_specs=[SMEM] + [VMEM] * (len(SENDS) + 3),
        out_specs=(VMEM, VMEM),
        scratch_shapes=[pltpu.VMEM((BLK // 2, 8, 8, 2 * RANK), jnp.float32)],
        compiler_params=LIMIT,
        cost_estimate=pl.CostEstimate(flops=4 * 64 * W * S, bytes_accessed=10 << 20, transcendentals=0),
        name="product",
    )(classes, *got, v, near, u)


def on_device(x_t, far_v, far_u, far_cols, rank_class, near_block):
    both = jnp.stack(
        [move(x_t, lambda z, y, x, c: ((2 * x + c + turn) % Z, y, z // 2, z % 2)) for turn in TURNS]
    )
    asked, kept, given = halves(far_cols, x_t)
    lines = [[z * Y + y for z in range(Z)] for y in range(Y)]
    asked = lax.all_to_all(asked, "rows", 0, 0, axis_index_groups=lines, tiled=True)
    sent = pick([along_y(both, m) for m in range(Y)], asked)
    own = own_piece(kept, given)
    got = [along_z(part, way) for part, (way, _) in zip(sent, SENDS)]
    near = near_product(own, near_block)
    keep, send = product(
        rank_class.reshape(BLK), got, far_v.reshape(BLK, RANK, W), near, far_u.reshape(BLK * RANK, S)
    )
    both = keep + other_core(send).astype(jnp.float32)
    parts = [across_x(both[8 * j:8 * j + 8].astype(jnp.bfloat16), j) for j in (2, 1, 3)]
    total = both[:8]
    for part in parts:
        total = total + part.astype(jnp.float32)
    return total.astype(jnp.bfloat16)


def solution(mesh):
    in_specs = (
        P("rhs", "rows"),
        P("rows", "rhs", None, None),
        P("rows", "rhs", None, None),
        P("rows", "rhs"),
        P("rows", "rhs"),
        P("rows", "rhs"),
    )
    return jax.shard_map(on_device, mesh=mesh, in_specs=in_specs, out_specs=P("rhs", "rows"), check_vma=False)
```

```python
import jax
import jax.numpy as jnp
from jax import lax
from jax.experimental import pallas as pl
from jax.experimental.pallas import tpu as pltpu
from jax.sharding import PartitionSpec as P

Z, Y, X, C = 8, 4, 4, 2
PIECES, BLK, RANK, W, S = 8, 8, 64, 512, 4096
AXES = ("rows", "rhs")
NT = (((1,), (1,)), ((), ()))
NN = (((1,), (0,)), ((), ()))
TILE = 512
VMEM, SMEM = pl.BlockSpec(memory_space=pltpu.VMEM), pl.BlockSpec(memory_space=pltpu.SMEM)
TURNS = (0, 4)
SENDS = ((0, (0, 1)), (2, (0, 1)), (1, (0, 1)), (-1, (0, 1)))
LONG = pl.CostEstimate(flops=20 << 30, bytes_accessed=1 << 20, transcendentals=0)
LIMIT = pltpu.CompilerParams(vmem_limit_bytes=8 << 20)


def bf16(*shape):
    return jax.ShapeDtypeStruct(shape, jnp.bfloat16)


def f32(*shape):
    return jax.ShapeDtypeStruct(shape, jnp.float32)


def pairs(target):
    place = lambda z, y, x, c: ((z * Y + y) * X + x) * C + c
    return [
        (place(z, y, x, c), place(*target(z, y, x, c)))
        for z in range(Z) for y in range(Y) for x in range(X) for c in range(C)
    ]


def move(part, target):
    return lax.ppermute(part, AXES, pairs(target))


def turned(way, core):
    return way * (1 - 2 * core) if way == 2 else way


def send_z(part, way):
    return move(part, lambda z, y, x, c: ((z + turned(way, c)) % Z, y, x, c))


def ask_z(part, way):
    return move(part, lambda z, y, x, c: ((z - turned(way, c)) % Z, y, x, c))


def across_x(part, j):
    return move(part, lambda z, y, x, c: (z, y, x ^ j, c))


def along_y(part, m):
    return part if m == 0 else move(part, lambda z, y, x, c: (z, (y + m) % Y, x, c))


def other_core(part):
    return move(part, lambda z, y, x, c: (z, y, x, 1 - c))


def pick_kernel(*refs):
    n = len(SENDS)
    held_refs, asked_refs, out_refs, held_ref = refs[:Y], refs[Y:Y + n], refs[Y + n:-1], refs[-1]
    y, core = lax.axis_index("rows") & 3, lax.axis_index("rhs") & 1
    for m in range(Y):
        held_ref[m] = held_refs[m][...]
    for (way, parts), asked_ref, out_ref in zip(SENDS, asked_refs, out_refs):
        for b in range(BLK):
            piece = asked_ref[0, b]
            source = (y - (piece >> 3)) & 3
            cols = pl.ds(pl.multiple_of((piece & 7) * W, W), W)
            for n, part in enumerate(parts):
                out_ref[n, b] = held_ref[source, part ^ core if way == 2 else part, :, cols]


def pick(held, asked):
    return pl.pallas_call(
        pick_kernel,
        out_shape=[bf16(len(parts), BLK, 8, W) for _, parts in SENDS],
        in_specs=[VMEM] * Y + [SMEM] * len(SENDS),
        out_specs=[VMEM] * len(SENDS),
        scratch_shapes=[pltpu.VMEM((Y, len(TURNS), 8, PIECES * W), jnp.bfloat16)],
        compiler_params=LIMIT,
        cost_estimate=LONG,
        name="pick",
    )(*held, *asked)


def halves_kernel(x_ref, mine_ref, yours_ref):
    k = lax.axis_index("rhs")
    x, core = k >> 1, k & 1
    for j in range(X):
        for c, ref in ((core, mine_ref), (1 - core, yours_ref)):
            start = pl.multiple_of(((x ^ j) * 2 + c) * W, W)
            ref[j] = x_ref[:, pl.ds(start, W)]


def halves(x_t):
    return pl.pallas_call(
        halves_kernel,
        out_shape=[bf16(X, 8, W)] * 2,
        in_specs=[VMEM],
        out_specs=[VMEM] * 2,
        compiler_params=LIMIT,
        cost_estimate=LONG,
        name="halves",
    )(x_t)


def own_piece(mine, yours):
    parts = jnp.stack([mine, other_core(yours)], 1)
    far = across_x(parts[2:], 2)
    near = across_x(jnp.stack([parts[1], far[1]]), 1)
    return [parts[0], near[0], far[0], near[1]]


def near_kernel(*refs):
    x_refs, (near_ref, out_ref) = refs[:-2], refs[-2:]
    x = jnp.concatenate([r[c].astype(jnp.float32) for c in range(C) for r in x_refs], 0).astype(jnp.bfloat16)
    for t in range(0, S, TILE):
        out_ref[:, t:t + TILE] = lax.dot_general(
            x, near_ref[t:t + TILE, :], NT, preferred_element_type=jnp.float32
        )


def near_product(own, near):
    return pl.pallas_call(
        near_kernel,
        out_shape=f32(64, S),
        in_specs=[VMEM] * (X + 1),
        out_specs=VMEM,
        compiler_params=LIMIT,
        cost_estimate=pl.CostEstimate(flops=2 * 64 * W * S, bytes_accessed=5 << 20, transcendentals=0),
        name="near",
    )(*own, near)


def product_kernel(cls_ref, *refs):
    got_refs, (v_ref, near_ref, u_ref, keep_ref, send_ref, z_buf) = refs[:len(SENDS)], refs[len(SENDS):]
    k, depth = lax.axis_index("rhs"), lax.axis_index("rows") >> 2
    x, core = k >> 1, k & 1
    got = {
        (-way - TURNS[part]) & 7: (ref, n)
        for ref, (way, parts) in zip(got_refs, SENDS) for n, part in enumerate(parts)
    }
    ranks = lax.broadcasted_iota(jnp.int32, (64, RANK), 1)
    halves = []
    for b in range(BLK):
        block = jnp.concatenate([got[d][0][got[d][1], b].astype(jnp.float32) for d in range(Z)], 0).astype(jnp.bfloat16)
        z = lax.dot_general(block, v_ref[b], NT, preferred_element_type=jnp.float32)
        rank = jnp.where(cls_ref[b] == 0, RANK // 4, jnp.where(cls_ref[b] == 1, RANK // 2, RANK))
        halves.append(jnp.where(ranks < rank, z, 0.0))
    for b in range(0, BLK, 2):
        z_buf[b // 2] = jnp.concatenate(halves[b:b + 2], 1).reshape(8, 8, 2 * RANK)
    order = [(x ^ j) * 2 + core for j in range(X)] + [(x ^ j) * 2 + 1 - core for j in range(X)]
    zmask = jnp.concatenate(
        [jnp.concatenate([z_buf[j, (place - depth) & 7] for place in order], 0) for j in range(BLK // 2)], 1
    ).astype(jnp.bfloat16)
    for t in range(0, S, TILE):
        cols = slice(t, t + TILE)
        y = near_ref[:, cols] + lax.dot_general(zmask, u_ref[:, cols], NN, preferred_element_type=jnp.float32)
        keep_ref[:, cols] = y[:32]
        send_ref[:, cols] = y[32:].astype(jnp.bfloat16)


def product(classes, got, v, near, u):
    return pl.pallas_call(
        product_kernel,
        out_shape=(f32(32, S), bf16(32, S)),
        in_specs=[SMEM] + [VMEM] * (len(SENDS) + 3),
        out_specs=(VMEM, VMEM),
        scratch_shapes=[pltpu.VMEM((BLK // 2, 8, 8, 2 * RANK), jnp.float32)],
        compiler_params=LIMIT,
        cost_estimate=pl.CostEstimate(flops=4 * 64 * W * S, bytes_accessed=10 << 20, transcendentals=0),
        name="product",
    )(classes, *got, v, near, u)


def on_device(x_t, far_v, far_u, far_cols, rank_class, near_block):
    both = jnp.stack(
        [move(x_t, lambda z, y, x, c: ((2 * x + c + turn) % Z, y, z // 2, z % 2)) for turn in TURNS]
    )
    own = own_piece(*halves(x_t))
    both, asked = lax.optimization_barrier((both, far_cols))
    asked = [asked if way == 0 else ask_z(asked, way) for way, _ in SENDS]
    sent = pick([along_y(both, m) for m in range(Y)], asked)
    got = [part if way == 0 else send_z(part, way) for part, (way, _) in zip(sent, SENDS)]
    near = near_product(own, near_block)
    keep, send = product(
        rank_class.reshape(BLK), got, far_v.reshape(BLK, RANK, W), near, far_u.reshape(BLK * RANK, S)
    )
    both = keep + other_core(send).astype(jnp.float32)
    parts = [across_x(both[8 * j:8 * j + 8].astype(jnp.bfloat16), j) for j in (2, 1, 3)]
    total = both[:8]
    for part in parts:
        total = total + part.astype(jnp.float32)
    return total.astype(jnp.bfloat16)


def solution(mesh):
    in_specs = (
        P("rhs", "rows"),
        P("rows", "rhs", None, None),
        P("rows", "rhs", None, None),
        P("rows", "rhs"),
        P("rows", "rhs"),
        P("rows", "rhs"),
    )
    return jax.shard_map(on_device, mesh=mesh, in_specs=in_specs, out_specs=P("rhs", "rows"), check_vma=False)
```

```python
import jax
import jax.numpy as jnp
from jax import lax
from jax.experimental import pallas as pl
from jax.experimental.pallas import tpu as pltpu
from jax.sharding import PartitionSpec as P

Z, Y, X, C = 8, 4, 4, 2
PIECES, BLK, RANK, W, S = 8, 8, 64, 512, 4096
AXES = ("rows", "rhs")
NT = (((1,), (1,)), ((), ()))
NN = (((1,), (0,)), ((), ()))
TILE = 512
VMEM, SMEM = pl.BlockSpec(memory_space=pltpu.VMEM), pl.BlockSpec(memory_space=pltpu.SMEM)
TURNS = (0, 4)
SENDS = ((0, (0, 1)), (2, (0, 1)), (1, (0, 1)), (-1, (0, 1)))
UPS = (0, 1, 3, 2)
LONG = pl.CostEstimate(flops=20 << 30, bytes_accessed=1 << 20, transcendentals=0)
LIMIT = pltpu.CompilerParams(vmem_limit_bytes=8 << 20)


def bf16(*shape):
    return jax.ShapeDtypeStruct(shape, jnp.bfloat16)


def f32(*shape):
    return jax.ShapeDtypeStruct(shape, jnp.float32)


def pairs(target):
    place = lambda z, y, x, c: ((z * Y + y) * X + x) * C + c
    return [
        (place(z, y, x, c), place(*target(z, y, x, c)))
        for z in range(Z) for y in range(Y) for x in range(X) for c in range(C)
    ]


def move(part, target):
    return lax.ppermute(part, AXES, pairs(target))


def turned(way, core):
    return way * (1 - 2 * core) if way == 2 else way


def send_z(part, way):
    return move(part, lambda z, y, x, c: ((z + turned(way, c)) % Z, y, x, c))


def ask_z(part, way):
    return move(part, lambda z, y, x, c: ((z - turned(way, c)) % Z, y, x, c))


def across_x(part, j):
    return move(part, lambda z, y, x, c: (z, y, x ^ j, c))


def along_y(part, m):
    return part if m == 0 else move(part, lambda z, y, x, c: (z, (y + m) % Y, x, c))


def other_core(part):
    return move(part, lambda z, y, x, c: (z, y, x, 1 - c))


def pick_kernel(*refs):
    n = len(SENDS)
    held_refs, asked_refs, out_refs, held_ref = refs[:Y], refs[Y:Y + n], refs[Y + n:-1], refs[-1]
    y, core = lax.axis_index("rows") & 3, lax.axis_index("rhs") & 1
    for m, ref in zip(UPS, held_refs):
        held_ref[m] = ref[...]
    for (way, parts), asked_ref, out_ref in zip(SENDS, asked_refs, out_refs):
        for b in range(BLK):
            piece = asked_ref[0, b]
            source = (y - (piece >> 3)) & 3
            cols = pl.ds(pl.multiple_of((piece & 7) * W, W), W)
            for n, part in enumerate(parts):
                out_ref[n, b] = held_ref[source, part ^ core if way == 2 else part, :, cols]


def pick(held, asked):
    return pl.pallas_call(
        pick_kernel,
        out_shape=[bf16(len(parts), BLK, 8, W) for _, parts in SENDS],
        in_specs=[VMEM] * Y + [SMEM] * len(SENDS),
        out_specs=[VMEM] * len(SENDS),
        scratch_shapes=[pltpu.VMEM((Y, len(TURNS), 8, PIECES * W), jnp.bfloat16)],
        compiler_params=LIMIT,
        cost_estimate=LONG,
        name="pick",
    )(*held, *asked)


def halves_kernel(x_ref, mine_ref, yours_ref):
    k = lax.axis_index("rhs")
    x, core = k >> 1, k & 1
    for j in range(X):
        for c, ref in ((core, mine_ref), (1 - core, yours_ref)):
            start = pl.multiple_of(((x ^ j) * 2 + c) * W, W)
            ref[j] = x_ref[:, pl.ds(start, W)]


def halves(x_t):
    return pl.pallas_call(
        halves_kernel,
        out_shape=[bf16(X, 8, W)] * 2,
        in_specs=[VMEM],
        out_specs=[VMEM] * 2,
        compiler_params=LIMIT,
        cost_estimate=LONG,
        name="halves",
    )(x_t)


def own_piece(mine, yours):
    parts = jnp.stack([mine, other_core(yours)], 1)
    far = across_x(parts[2:], 2)
    near = across_x(jnp.stack([parts[1], far[1]]), 1)
    return [parts[0], near[0], far[0], near[1]]


def near_kernel(*refs):
    x_refs, (near_ref, out_ref) = refs[:-2], refs[-2:]
    x = jnp.concatenate([r[c].astype(jnp.float32) for c in range(C) for r in x_refs], 0).astype(jnp.bfloat16)
    for t in range(0, S, TILE):
        out_ref[:, t:t + TILE] = lax.dot_general(
            x, near_ref[t:t + TILE, :], NT, preferred_element_type=jnp.float32
        )


def near_product(own, near):
    return pl.pallas_call(
        near_kernel,
        out_shape=f32(64, S),
        in_specs=[VMEM] * (X + 1),
        out_specs=VMEM,
        compiler_params=LIMIT,
        cost_estimate=pl.CostEstimate(flops=2 * 64 * W * S, bytes_accessed=5 << 20, transcendentals=0),
        name="near",
    )(*own, near)


def product_kernel(cls_ref, *refs):
    got_refs, (v_ref, near_ref, u_ref, keep_ref, send_ref, z_buf) = refs[:len(SENDS)], refs[len(SENDS):]
    k, depth = lax.axis_index("rhs"), lax.axis_index("rows") >> 2
    x, core = k >> 1, k & 1
    got = {
        (-way - TURNS[part]) & 7: (ref, n)
        for ref, (way, parts) in zip(got_refs, SENDS) for n, part in enumerate(parts)
    }
    ranks = lax.broadcasted_iota(jnp.int32, (64, RANK), 1)
    halves = []
    for b in range(BLK):
        block = jnp.concatenate([got[d][0][got[d][1], b].astype(jnp.float32) for d in range(Z)], 0).astype(jnp.bfloat16)
        z = lax.dot_general(block, v_ref[b], NT, preferred_element_type=jnp.float32)
        rank = jnp.where(cls_ref[b] == 0, RANK // 4, jnp.where(cls_ref[b] == 1, RANK // 2, RANK))
        halves.append(jnp.where(ranks < rank, z, 0.0))
    for b in range(0, BLK, 2):
        z_buf[b // 2] = jnp.concatenate(halves[b:b + 2], 1).reshape(8, 8, 2 * RANK)
    order = [(x ^ j) * 2 + core for j in range(X)] + [(x ^ j) * 2 + 1 - core for j in range(X)]
    zmask = jnp.concatenate(
        [jnp.concatenate([z_buf[j, (place - depth) & 7] for place in order], 0) for j in range(BLK // 2)], 1
    ).astype(jnp.bfloat16)
    for t in range(0, S, TILE):
        cols = slice(t, t + TILE)
        y = near_ref[:, cols] + lax.dot_general(zmask, u_ref[:, cols], NN, preferred_element_type=jnp.float32)
        keep_ref[:, cols] = y[:32]
        send_ref[:, cols] = y[32:].astype(jnp.bfloat16)


def product(classes, got, v, near, u):
    return pl.pallas_call(
        product_kernel,
        out_shape=(f32(32, S), bf16(32, S)),
        in_specs=[SMEM] + [VMEM] * (len(SENDS) + 3),
        out_specs=(VMEM, VMEM),
        scratch_shapes=[pltpu.VMEM((BLK // 2, 8, 8, 2 * RANK), jnp.float32)],
        compiler_params=LIMIT,
        cost_estimate=pl.CostEstimate(flops=4 * 64 * W * S, bytes_accessed=10 << 20, transcendentals=0),
        name="product",
    )(classes, *got, v, near, u)


def on_device(x_t, far_v, far_u, far_cols, rank_class, near_block):
    both = jnp.stack(
        [move(x_t, lambda z, y, x, c: ((2 * x + c + turn) % Z, y, z // 2, z % 2)) for turn in TURNS]
    )
    own = own_piece(*halves(x_t))
    both, asked = lax.optimization_barrier((both, far_cols))
    asked = [asked if way == 0 else ask_z(asked, way) for way, _ in SENDS]
    sent = pick([along_y(both, m) for m in UPS], asked)
    got = [part if way == 0 else send_z(part, way) for part, (way, _) in zip(sent, SENDS)]
    near = near_product(own, near_block)
    keep, send = product(
        rank_class.reshape(BLK), got, far_v.reshape(BLK, RANK, W), near, far_u.reshape(BLK * RANK, S)
    )
    both = keep + other_core(send).astype(jnp.float32)
    parts = [across_x(both[8 * j:8 * j + 8].astype(jnp.bfloat16), j) for j in (2, 1, 3)]
    total = both[:8]
    for part in parts:
        total = total + part.astype(jnp.float32)
    return total.astype(jnp.bfloat16)


def solution(mesh):
    in_specs = (
        P("rhs", "rows"),
        P("rows", "rhs", None, None),
        P("rows", "rhs", None, None),
        P("rows", "rhs"),
        P("rows", "rhs"),
        P("rows", "rhs"),
    )
    return jax.shard_map(on_device, mesh=mesh, in_specs=in_specs, out_specs=P("rhs", "rows"), check_vma=False)
```

```python
import jax
import jax.numpy as jnp
from jax import lax
from jax.experimental import pallas as pl
from jax.experimental.pallas import tpu as pltpu
from jax.sharding import PartitionSpec as P

Z, Y, X, C = 8, 4, 4, 2
PIECES, BLK, RANK, W, S = 8, 8, 64, 512, 4096
AXES = ("rows", "rhs")
NT = (((1,), (1,)), ((), ()))
NN = (((1,), (0,)), ((), ()))
TILE = 512
VMEM, SMEM = pl.BlockSpec(memory_space=pltpu.VMEM), pl.BlockSpec(memory_space=pltpu.SMEM)
TURNS = (0, 4)
SENDS = ((0, (0, 1)), (2, (0, 1)), (1, (0, 1)), (-1, (0, 1)))
UPS = (0, 1, 3, 2)
LONG = pl.CostEstimate(flops=20 << 30, bytes_accessed=1 << 20, transcendentals=0)
LIMIT = pltpu.CompilerParams(vmem_limit_bytes=8 << 20)


def bf16(*shape):
    return jax.ShapeDtypeStruct(shape, jnp.bfloat16)


def f32(*shape):
    return jax.ShapeDtypeStruct(shape, jnp.float32)


def pairs(target):
    place = lambda z, y, x, c: ((z * Y + y) * X + x) * C + c
    return [
        (place(z, y, x, c), place(*target(z, y, x, c)))
        for z in range(Z) for y in range(Y) for x in range(X) for c in range(C)
    ]


def move(part, target):
    return lax.ppermute(part, AXES, pairs(target))


def turned(way, core):
    return way * (1 - 2 * core) if way == 2 else way


def send_z(part, way):
    return move(part, lambda z, y, x, c: ((z + turned(way, c)) % Z, y, x, c))


def ask_z(part, way):
    return move(part, lambda z, y, x, c: ((z - turned(way, c)) % Z, y, x, c))


def across_x(part, j):
    return move(part, lambda z, y, x, c: (z, y, x ^ j, c))


def along_y(part, m):
    return part if m == 0 else move(part, lambda z, y, x, c: (z, (y + m) % Y, x, c))


def other_core(part):
    return move(part, lambda z, y, x, c: (z, y, x, 1 - c))


def pick_kernel(*refs):
    n = len(SENDS)
    held_refs, asked_refs, out_refs, held_ref = refs[:Y], refs[Y:Y + n], refs[Y + n:-1], refs[-1]
    y, core = lax.axis_index("rows") & 3, lax.axis_index("rhs") & 1
    for m, ref in zip(UPS, held_refs):
        held_ref[m] = ref[...]
    for (way, parts), asked_ref, out_ref in zip(SENDS, asked_refs, out_refs):
        for b in range(BLK):
            piece = asked_ref[0, b]
            source = (y - (piece >> 3)) & 3
            cols = pl.ds(pl.multiple_of((piece & 7) * W, W), W)
            for n, part in enumerate(parts):
                out_ref[n, b] = held_ref[source, part ^ core if way == 2 else part, :, cols]


def pick(held, asked):
    return pl.pallas_call(
        pick_kernel,
        out_shape=[bf16(len(parts), BLK, 8, W) for _, parts in SENDS],
        in_specs=[VMEM] * Y + [SMEM] * len(SENDS),
        out_specs=[VMEM] * len(SENDS),
        scratch_shapes=[pltpu.VMEM((Y, len(TURNS), 8, PIECES * W), jnp.bfloat16)],
        compiler_params=LIMIT,
        cost_estimate=LONG,
        name="pick",
    )(*held, *asked)


def halves_kernel(x_ref, mine_ref, yours_ref):
    k = lax.axis_index("rhs")
    x, core = k >> 1, k & 1
    for j in range(X):
        for c, ref in ((core, mine_ref), (1 - core, yours_ref)):
            start = pl.multiple_of(((x ^ j) * 2 + c) * W, W)
            ref[j] = x_ref[:, pl.ds(start, W)]


def halves(x_t):
    return pl.pallas_call(
        halves_kernel,
        out_shape=[bf16(X, 8, W)] * 2,
        in_specs=[VMEM],
        out_specs=[VMEM] * 2,
        compiler_params=LIMIT,
        cost_estimate=LONG,
        name="halves",
    )(x_t)


def own_piece(mine, theirs):
    parts = jnp.stack([mine, theirs], 1)
    far = across_x(parts[2:], 2)
    near = across_x(jnp.stack([parts[1], far[1]]), 1)
    return [parts[0], near[0], far[0], near[1]]


def near_kernel(*refs):
    x_refs, (near_ref, out_ref) = refs[:-2], refs[-2:]
    x = jnp.concatenate([r[c].astype(jnp.float32) for c in range(C) for r in x_refs], 0).astype(jnp.bfloat16)
    for t in range(0, S, TILE):
        out_ref[:, t:t + TILE] = lax.dot_general(
            x, near_ref[t:t + TILE, :], NT, preferred_element_type=jnp.float32
        )


def near_product(own, near):
    return pl.pallas_call(
        near_kernel,
        out_shape=f32(64, S),
        in_specs=[VMEM] * (X + 1),
        out_specs=VMEM,
        compiler_params=LIMIT,
        cost_estimate=pl.CostEstimate(flops=2 * 64 * W * S, bytes_accessed=5 << 20, transcendentals=0),
        name="near",
    )(*own, near)


def product_kernel(cls_ref, *refs):
    got_refs, (v_ref, near_ref, u_ref, keep_ref, send_ref, z_buf) = refs[:len(SENDS)], refs[len(SENDS):]
    k, depth = lax.axis_index("rhs"), lax.axis_index("rows") >> 2
    x, core = k >> 1, k & 1
    got = {
        (-way - TURNS[part]) & 7: (ref, n)
        for ref, (way, parts) in zip(got_refs, SENDS) for n, part in enumerate(parts)
    }
    ranks = lax.broadcasted_iota(jnp.int32, (64, RANK), 1)
    halves = []
    for b in range(BLK):
        block = jnp.concatenate([got[d][0][got[d][1], b].astype(jnp.float32) for d in range(Z)], 0).astype(jnp.bfloat16)
        z = lax.dot_general(block, v_ref[b], NT, preferred_element_type=jnp.float32)
        rank = jnp.where(cls_ref[b] == 0, RANK // 4, jnp.where(cls_ref[b] == 1, RANK // 2, RANK))
        halves.append(jnp.where(ranks < rank, z, 0.0))
    for b in range(0, BLK, 2):
        z_buf[b // 2] = jnp.concatenate(halves[b:b + 2], 1).reshape(8, 8, 2 * RANK)
    order = [(x ^ j) * 2 + core for j in range(X)] + [(x ^ j) * 2 + 1 - core for j in range(X)]
    zmask = jnp.concatenate(
        [jnp.concatenate([z_buf[j, (place - depth) & 7] for place in order], 0) for j in range(BLK // 2)], 1
    ).astype(jnp.bfloat16)
    for t in range(0, S, TILE):
        cols = slice(t, t + TILE)
        y = near_ref[:, cols] + lax.dot_general(zmask, u_ref[:, cols], NN, preferred_element_type=jnp.float32)
        keep_ref[:, cols] = y[:32]
        send_ref[:, cols] = y[32:].astype(jnp.bfloat16)


def product(classes, got, v, near, u):
    return pl.pallas_call(
        product_kernel,
        out_shape=(f32(32, S), bf16(32, S)),
        in_specs=[SMEM] + [VMEM] * (len(SENDS) + 3),
        out_specs=(VMEM, VMEM),
        scratch_shapes=[pltpu.VMEM((BLK // 2, 8, 8, 2 * RANK), jnp.float32)],
        compiler_params=LIMIT,
        cost_estimate=pl.CostEstimate(flops=4 * 64 * W * S, bytes_accessed=10 << 20, transcendentals=0),
        name="product",
    )(classes, *got, v, near, u)


def on_device(x_t, far_v, far_u, far_cols, rank_class, near_block):
    both = jnp.stack(
        [move(x_t, lambda z, y, x, c: ((2 * x + c + turn) % Z, y, z // 2, z % 2)) for turn in TURNS]
    )
    kept, given = halves(x_t)
    theirs, early = lax.optimization_barrier((other_core(given), far_cols))
    own = own_piece(kept, theirs)
    soon = ask_z(early, 2)
    both, asked, soon = lax.optimization_barrier((both, far_cols, soon))
    asked = [soon if way == 2 else asked if way == 0 else ask_z(asked, way) for way, _ in SENDS]
    sent = pick([along_y(both, m) for m in UPS], asked)
    got = [part if way == 0 else send_z(part, way) for part, (way, _) in zip(sent, SENDS)]
    near = near_product(own, near_block)
    keep, send = product(
        rank_class.reshape(BLK), got, far_v.reshape(BLK, RANK, W), near, far_u.reshape(BLK * RANK, S)
    )
    both = keep + other_core(send).astype(jnp.float32)
    parts = [across_x(both[8 * j:8 * j + 8].astype(jnp.bfloat16), j) for j in (2, 1, 3)]
    total = both[:8]
    for part in parts:
        total = total + part.astype(jnp.float32)
    return total.astype(jnp.bfloat16)


def solution(mesh):
    in_specs = (
        P("rhs", "rows"),
        P("rows", "rhs", None, None),
        P("rows", "rhs", None, None),
        P("rows", "rhs"),
        P("rows", "rhs"),
        P("rows", "rhs"),
    )
    return jax.shard_map(on_device, mesh=mesh, in_specs=in_specs, out_specs=P("rhs", "rows"), check_vma=False)
```
